512 devices in a mesh: col: 128 (over y, z, core), row: 4 (over x).
Axes of the slice: x: 4, y: 8, z: 8, core: 2. Of those that a mesh axis runs over, the one named last changes fastest.
Arguments:
- factor: float32 [128, 512, 1024], P('col', 'row'), may hold values from -0.6 to 0.6
- pattern: int32 [128, 4, 8], replicated, may hold values from 0 to 1, as said below
- order: int32 [128], replicated, may hold values from 0 to 127, each once
- targets: int32 [2, 2], replicated, may hold values from 0 to 3, as said below
- panels: float32 [512, 512], P('row'), may hold values from -6 to 6
Outputs:
- carried: float32 [128, 512, 512], P('col', 'row')
The draws below stay inside these ranges and needn't reach their ends.
Inputs may be any that keep to these rules, and one draw needn't show every extreme that they name: `pattern`: 0 or 1 for each block of a supernode's rows and factored columns; the share of present blocks differs between supernodes. `targets`: every row block 0..3 is named at least once.
All inputs are finite; a program needn't handle non-finite values.
Results may differ from the reference program's by a relative error of at most 0.0001.
Values sent between devices are 32-bit elements; how exact they have to be, the bound alone decides.
A program may use at most 128 MiB of HBM per device.

```python
import jax
import jax.numpy as jnp
from jax import lax

BLOCK = 128
F = 1024
PANEL = 256
NP = 2
R_DEV = 128
ROWS = 512
N_COL = 128


def draw_pattern(key, part):
    first_key, second_key = jax.random.split(key)
    shares = jax.random.randint(first_key, (N_COL, 1, 1), 3, 8)
    cells = jax.random.randint(second_key, (N_COL, ROWS // BLOCK, F // BLOCK), 0, 10)
    return (cells < shares).astype(jnp.int32)


def draw_targets(key, part):
    slots = NP * (PANEL // BLOCK)
    owners = ROWS // R_DEV
    per_owner = R_DEV // BLOCK
    shuffled = jax.random.permutation(jax.random.fold_in(key, 3), slots)
    within = jax.random.randint(jax.random.fold_in(key, 7), (slots,), 0, per_owner)
    owner_of = shuffled % owners
    slot_ids = jnp.arange(slots, dtype=jnp.int32)
    top_slot = jnp.argmax((owner_of == owners - 1).astype(jnp.int32))
    bottom_slot = slots - 1 - jnp.argmax(jnp.flip((owner_of == 0).astype(jnp.int32)))
    within = jnp.where(slot_ids == top_slot, per_owner - 1, within)
    within = jnp.where(slot_ids == bottom_slot, 0, within)
    chosen = owner_of * per_owner + within
    return chosen.reshape(NP, PANEL // BLOCK).astype(jnp.int32)


def block_levels(own_key, shape, pieces, least, largest):
    loudness = 1.0
    for dim, shards_of in pieces:
        draws = jax.random.uniform(jax.random.fold_in(jax.random.fold_in(own_key, 6), dim), (shards_of,), jnp.float32, least / len(pieces), largest / len(pieces))
        loudness = loudness * jnp.repeat(jnp.exp(draws), shape[dim] // shards_of).reshape((-1,) + (1,) * (len(shape) - 1 - dim))
    return loudness


def noise(rng, dims, width, reach, cuts=(), kind=jnp.bfloat16):
    loudness = block_levels(rng, dims, cuts, -0.22, 0.18) if cuts else 1.0
    result = jax.random.normal(rng, dims, jnp.float32) * width * loudness
    return jnp.minimum(jnp.maximum(result, -reach), reach).astype(kind)


def setup_inputs(seed: int = 0) -> dict:
    key_list = jax.random.split(jax.random.key(seed), 6)
    factor = noise(key_list[0], (N_COL, ROWS, F), 0.09, 0.6, ((0, 128), (1, 4)), jnp.float32)
    pattern = draw_pattern(jax.random.fold_in(key_list[5], 71), 0)
    order = jax.random.permutation(key_list[2], N_COL).astype(jnp.int32)
    targets = draw_targets(jax.random.fold_in(key_list[5], 71), 0)
    panels = noise(key_list[4], (ROWS, NP * PANEL), 1.0, 6.0, ((0, 4),), jnp.float32)
    return {"factor": factor, "pattern": pattern, "order": order, "targets": targets, "panels": panels}


def reference(factor, pattern, order, targets, panels):
    row_blocks = ROWS // BLOCK
    col_blocks = F // BLOCK

    def step(state, inputs):
        owner_rows, position = inputs
        supernode = order[position]
        present = pattern[supernode].astype(jnp.float32)
        masked = (owner_rows.reshape(row_blocks, BLOCK, col_blocks, BLOCK) * present[:, None, :, None]).reshape(ROWS, F)
        strips = jnp.take(masked.reshape(row_blocks, BLOCK, F), targets.reshape(-1), axis=0).reshape(NP * PANEL, F)
        update = lax.dot_general(masked, strips, (((1,), (1,)), ((), ())), precision=lax.Precision.HIGHEST, preferred_element_type=jnp.float32)
        state = state - update
        return state, state

    _, carried = lax.scan(step, panels, (factor, jnp.arange(N_COL, dtype=jnp.int32)))
    return carried
```

```python
import jax
import jax.numpy as jnp
from jax import lax
from jax.experimental import pallas as pl
from jax.experimental.pallas import tpu as pltpu
from jax.sharding import Mesh
from jax.sharding import PartitionSpec as P

BLOCK = 128
TILE = 8
NX, NY, NZ, NC = 4, 8, 8, 2
NQ = NZ * NC
MESH = pl.DeviceIdType.MESH
COL = ("y", "z", "core")
OWN, NEAR, FAR = 0, 1, 2


def split(value):
    high = value.astype(jnp.bfloat16)
    return high, (value - high.astype(jnp.float32)).astype(jnp.bfloat16)


def product(ah, al, bh, bl):
    def dot(a, b):
        return lax.dot_general(
            a, b, (((1,), (1,)), ((), ())), preferred_element_type=jnp.float32
        )

    return dot(ah, bh) + (dot(ah, bl) + dot(al, bh))


def kernel(
    order_ref, targets_ref, pattern_ref, factor_ref, panels_ref, out_ref,
    own, near, far, high, low, fhigh, flow, mask, pan,
    u, f, tot, yb, e, ret, rt,
    heavy_send, heavy_recv, local_sem,
    fwd_send, fwd_recv, y_send, y_recv, ret_send, ret_recv, rt_send, rt_recv,
):
    x, y, z, c = (lax.axis_index(a) for a in ("x", "y", "z", "core"))
    q = z * NC + c
    position = y * NQ + q
    ahead = lax.rem(x + 1 + 2 * c, NX)
    behind = lax.rem(x + 3 + 2 * c, NX)
    up, down, across = lax.rem(x + 1, NX), lax.rem(x + 3, NX), lax.rem(x + 2, NX)

    def at(x_, y_, q_):
        return (y_, q_ // NC, lax.rem(q_, NC), x_)

    def half(row):
        return pl.ds(pl.multiple_of((row // 2) * 512, 512), 512)

    def other(row):
        return pl.ds(pl.multiple_of((1 - row // 2) * 512, 512), 512)

    load_own = pltpu.make_async_copy(factor_ref.at[0], own, local_sem.at[0])
    load_pan = pltpu.make_async_copy(panels_ref, pan, local_sem.at[1])
    load_own.start()
    load_pan.start()

    with jax.named_scope("barrier"):
        barrier = pltpu.get_barrier_semaphore()
        for k in range(1, NX):
            pl.semaphore_signal(barrier, inc=1, device_id=at(lax.rem(x + k, NX), y, q), device_id_type=MESH)
        for k in range(1, NQ):
            pl.semaphore_signal(barrier, inc=1, device_id=at(x, y, lax.rem(q + k, NQ)), device_id_type=MESH)
        for k in range(1, NY):
            pl.semaphore_signal(barrier, inc=1, device_id=at(x, lax.rem(y + k, NY), q), device_id_type=MESH)
        pl.semaphore_wait(barrier, NX + NQ + NY - 3)

    def heavy(src, dst, i):
        return pltpu.make_async_remote_copy(
            src_ref=src, dst_ref=dst, send_sem=heavy_send.at[i], recv_sem=heavy_recv.at[i],
            device_id=at(ahead, y, q), device_id_type=MESH,
        )

    first = heavy(factor_ref.at[0, :, half(x)], near.at[:, half(x)], 0)
    second = heavy(factor_ref.at[0, :, other(x)], near.at[:, other(x)], 1)
    relay = heavy(near.at[:, half(behind)], far, 2)
    first.start()
    second.start()

    lanes = lax.broadcasted_iota(jnp.int32, (8, BLOCK), 1)
    picked = lanes == order_ref[position]
    for j in range(NX):
        kept = jnp.where(picked, pattern_ref[j], 0).astype(jnp.float32)
        mask[j] = jnp.broadcast_to(jnp.sum(kept, axis=1, keepdims=True), (8, BLOCK))

    def prepare(src, row, first_block, blocks, put):
        for k in range(blocks):
            columns = pl.ds(k * BLOCK, BLOCK)
            masked = src[:, columns] * mask[row, pl.ds(first_block + k, 1), :]
            put(columns, *split(masked))

    def put_at(slot):
        def put(columns, h, l):
            high[slot, :, columns] = h
            low[slot, :, columns] = l

        return put

    def put_far(columns, h, l):
        fhigh[:, columns] = h
        flow[:, columns] = l

    def keep(g, value):
        u[g] = value.reshape(NQ, TILE, BLOCK)

    def send_tiles(src, dst, send, recv, row, start):
        for k in range(start, NQ):
            peer = lax.rem(q + k, NQ)
            pltpu.make_async_remote_copy(
                src_ref=src.at[peer], dst_ref=dst.at[q], send_sem=send, recv_sem=recv,
                device_id=at(row, y, peer), device_id_type=MESH,
            ).start()

    def wait_tiles(buffer, count, sem):
        part = buffer.at[pl.ds(0, count)]
        pltpu.make_async_copy(part, part, sem).wait()

    def forward(g):
        send_tiles(u.at[g], f.at[g], fwd_send.at[g], fwd_recv.at[g], x, 1)
        f[g, q] = u[g, q]

    def scan(g):
        total = f[g, 0]
        e[g, 0] = total
        for s in range(1, NQ):
            total = total + f[g, s]
            e[g, s] = total
        tot[g] = total
        for k in range(1, NY):
            peer = lax.rem(y + k, NY)
            pltpu.make_async_remote_copy(
                src_ref=tot.at[g], dst_ref=yb.at[g, y], send_sem=y_send.at[g], recv_sem=y_recv.at[g],
                device_id=at(x, peer, q), device_id_type=MESH,
            ).start()

    def give_back(g):
        wait_tiles(yb.at[g], NY - 1, y_recv.at[g])
        before = jnp.zeros((TILE, BLOCK), jnp.float32)
        for k in range(NY):
            before = before + jnp.where(k < y, yb[g, k], 0.0)
        for s in range(NQ):
            e[g, s] = e[g, s] + before
        send_tiles(e.at[g], ret.at[g], ret_send.at[g], ret_recv.at[g], x, 1)
        ret[g, q] = e[g, q]

    load_own.wait()
    with jax.named_scope("own"):
        prepare(own, x, 0, 8, put_at(c))
        keep(OWN, product(high[c], low[c], high[c], low[c]))
        forward(OWN)
    with jax.named_scope("relay_start"):
        first.wait_recv()
        relay.start()
    with jax.named_scope("own_scan"):
        wait_tiles(f.at[OWN], NQ - 1, fwd_recv.at[OWN])
        scan(OWN)
    with jax.named_scope("own_back"):
        give_back(OWN)

    with jax.named_scope("near_wait"):
        second.wait_recv()
    with jax.named_scope("near"):
        prepare(near, behind, 0, 8, put_at(1 - c))
        keep(NEAR, product(high[0], low[0], high[1], low[1]))

        @pl.when(c == 0)
        def _():
            forward(NEAR)

        @pl.when(c == 1)
        def _():
            send_tiles(u.at[NEAR], f.at[NEAR], fwd_send.at[NEAR], fwd_recv.at[NEAR], up, 0)

    with jax.named_scope("far_wait"):
        relay.wait_recv()
    with jax.named_scope("far"):
        prepare(far, across, (across // 2) * 4, 4, put_far)
        keep(FAR, product(high[c, :, half(across)], low[c, :, half(across)], fhigh[...], flow[...]))
        forward(FAR)

    with jax.named_scope("near_scan"):
        @pl.when(c == 0)
        def _():
            wait_tiles(f.at[NEAR], NQ - 1, fwd_recv.at[NEAR])

        @pl.when(c == 1)
        def _():
            wait_tiles(f.at[NEAR], NQ, fwd_recv.at[NEAR])

        scan(NEAR)
    with jax.named_scope("far_scan"):
        wait_tiles(f.at[FAR], NQ - 1, fwd_recv.at[FAR])
        scan(FAR)
    with jax.named_scope("near_back"):
        give_back(NEAR)
        send_tiles(e.at[NEAR], rt.at[0], rt_send.at[0], rt_recv.at[0], down, 0)
    with jax.named_scope("far_back"):
        give_back(FAR)
        send_tiles(e.at[FAR], rt.at[1], rt_send.at[1], rt_recv.at[1], across, 0)

    with jax.named_scope("ret_wait"):
        load_pan.wait()
        for g in (OWN, NEAR, FAR):
            wait_tiles(ret.at[g], NQ - 1, ret_recv.at[g])
        for g in range(2):
            wait_tiles(rt.at[g], NQ, rt_recv.at[g])
    with jax.named_scope("final"):
        square = (BLOCK, BLOCK)
        ret[3] = rt[0].reshape(square).T.reshape(NQ, TILE, BLOCK)
        ret[FAR] = ret[FAR] + rt[1].reshape(square).T.reshape(NQ, TILE, BLOCK)
        for s in range(4):
            rows = targets_ref[s // 2, s % 2]
            away = lax.rem(x - rows + NX, NX)
            columns = pl.ds(s * BLOCK, BLOCK)
            out_ref[0, :, columns] = pan[:, columns] - ret[away].reshape(square)

    with jax.named_scope("drain"):
        first.wait_send()
        second.wait_send()
        relay.wait_send()
        wait_tiles(u.at[OWN], NQ - 1, fwd_send.at[OWN])

        @pl.when(c == 0)
        def _():
            wait_tiles(u.at[NEAR], NQ - 1, fwd_send.at[NEAR])

        @pl.when(c == 1)
        def _():
            wait_tiles(u.at[NEAR], NQ, fwd_send.at[NEAR])

        wait_tiles(u.at[FAR], NQ - 1, fwd_send.at[FAR])
        for g in (OWN, NEAR, FAR):
            wait_tiles(yb.at[g], NY - 1, y_send.at[g])
            wait_tiles(e.at[g], NQ - 1, ret_send.at[g])
        for g in range(2):
            wait_tiles(e.at[g + 1], NQ, rt_send.at[g])


def body(factor, pattern, order, targets, panels):
    vm, sem = pltpu.VMEM, pltpu.SemaphoreType.DMA
    f32, bf16 = jnp.float32, jnp.bfloat16
    rows, width = factor.shape[1:]
    tiles = (NQ, TILE, BLOCK)
    return pl.pallas_call(
        kernel,
        out_shape=jax.ShapeDtypeStruct((1, *panels.shape), f32),
        in_specs=[
            pl.BlockSpec(memory_space=pltpu.SMEM),
            pl.BlockSpec(memory_space=pltpu.SMEM),
            pl.BlockSpec(memory_space=pltpu.VMEM),
            pl.BlockSpec(memory_space=pl.ANY),
            pl.BlockSpec(memory_space=pl.ANY),
        ],
        out_specs=pl.BlockSpec(memory_space=pltpu.VMEM),
        scratch_shapes=[
            vm((rows, width), f32), vm((rows, width), f32), vm((rows, width // 2), f32),
            vm((2, rows, width), bf16), vm((2, rows, width), bf16),
            vm((rows, width // 2), bf16), vm((rows, width // 2), bf16),
            vm((NX, 8, BLOCK), f32), vm(panels.shape, f32),
            vm((3, *tiles), f32), vm((3, *tiles), f32), vm((3, TILE, BLOCK), f32),
            vm((3, NY, TILE, BLOCK), f32), vm((3, *tiles), f32), vm((4, *tiles), f32), vm((2, *tiles), f32),
            sem((3,)), sem((3,)), sem((2,)),
            sem((3,)), sem((3,)), sem((3,)), sem((3,)), sem((3,)), sem((3,)), sem((2,)), sem((2,)),
        ],
        compiler_params=pltpu.CompilerParams(
            collective_id=0, has_side_effects=True, vmem_limit_bytes=32 * 2**20
        ),
        name="fan_in",
    )(order, targets, jnp.transpose(pattern, (1, 2, 0)), factor, panels)


def solution(mesh):
    torus = Mesh(mesh.devices.reshape(NY, NZ, NC, NX), (*COL, "x"))
    in_specs = (P(COL, "x", None), P(), P(), P(), P("x", None))
    return jax.shard_map(
        body, mesh=torus, in_specs=in_specs, out_specs=P(COL, "x", None), check_vma=False
    )
```

```python
import jax
import jax.numpy as jnp
from jax import lax
from jax.experimental import pallas as pl
from jax.experimental.pallas import tpu as pltpu
from jax.sharding import Mesh
from jax.sharding import PartitionSpec as P

BLOCK = 128
NX, NY, NZ, NC = 4, 8, 8, 2
NQ = NZ * NC
NR = 16
ROWS = BLOCK // NR
BASE = 0 if NR == NQ else NQ - NR // 2
MESH = pl.DeviceIdType.MESH
COL = ("y", "z", "core")
OWN, NEAR, FAR = 0, 1, 2


def split(value):
    high = value.astype(jnp.bfloat16)
    return high, (value - high.astype(jnp.float32)).astype(jnp.bfloat16)


def product(ah, al, bh, bl):
    def dot(a, b):
        return lax.dot_general(
            a, b, (((1,), (1,)), ((), ())), preferred_element_type=jnp.float32
        )

    return dot(ah, bh) + (dot(ah, bl) + dot(al, bh))


def kernel(
    order_hbm, targets_hbm, pattern_hbm, factor_hbm, panels_hbm, out_ref,
    order_ref, targets_ref, pattern_ref, own, near, far, high, low, fhigh, flow, mask, pan,
    u, f, tot, yb, e, ret, rt,
    heavy_send, heavy_recv, local_sem,
    fwd_send, fwd_recv, y_send, y_recv, ret_send, ret_recv, rt_send, rt_recv,
):
    x, y, z, c = (lax.axis_index(a) for a in ("x", "y", "z", "core"))
    q = z * NC + c
    slot = lax.rem(q + NQ - BASE, NQ)
    scans = slot < NR
    position = y * NQ + q
    up, down, across = (lax.rem(x + k, NX) for k in (1, 3, 2))
    ahead = lax.rem(x + 1 + 2 * c, NX)
    behind = lax.rem(x + 3 + 2 * c, NX)

    def at(x_, y_, q_):
        return (y_, q_ // NC, lax.rem(q_, NC), x_)

    def scanner(j):
        return lax.rem(j + BASE, NQ)

    def half(row):
        return pl.ds(pl.multiple_of((row // 2) * 512, 512), 512)

    def other(row):
        return pl.ds(pl.multiple_of((1 - row // 2) * 512, 512), 512)

    loads = [
        pltpu.make_async_copy(a, b, local_sem.at[i])
        for i, (a, b) in enumerate((
            (factor_hbm.at[0], own), (order_hbm, order_ref), (pattern_hbm, pattern_ref),
            (targets_hbm, targets_ref), (panels_hbm, pan),
        ))
    ]
    for load in loads:
        load.start()

    barrier = pltpu.get_barrier_semaphore()

    def greet(device):
        pl.semaphore_signal(barrier, inc=1, device_id=device, device_id_type=MESH)

    for k in range(1, NX):
        greet(at(lax.rem(x + k, NX), y, q))
    for k in range(1, NQ):
        greet(at(x, y, lax.rem(q + k, NQ)))
    for k in range(1, NY):
        greet(at(x, lax.rem(y + k, NY), q))

    @pl.when(scans)
    def _():
        for k in range(NZ):
            greet(at(down, y, k * NC + 1))

    pl.semaphore_wait(barrier, NX + NQ + NY - 3 + c * NR)

    def exchange(src, dst, i, row):
        return pltpu.make_async_remote_copy(
            src_ref=src, dst_ref=dst, send_sem=heavy_send.at[i], recv_sem=heavy_recv.at[i],
            device_id=at(row, y, q), device_id_type=MESH,
        )

    first = exchange(factor_hbm.at[0, :, half(ahead)], near.at[:, half(ahead)], 0, ahead)
    second = exchange(factor_hbm.at[0, :, other(ahead)], near.at[:, other(ahead)], 1, ahead)
    third = exchange(factor_hbm.at[0, :, half(behind)], far, 2, behind)
    first.start()
    third.start()
    second.start()

    loads[1].wait()
    loads[2].wait()
    lanes = lax.broadcasted_iota(jnp.int32, (8, BLOCK), 1)
    picked = lanes == order_ref[position]
    for j in range(NX):
        kept = jnp.where(picked, pattern_ref[j], 0).astype(jnp.float32)
        mask[j] = jnp.broadcast_to(jnp.sum(kept, axis=1, keepdims=True), (8, BLOCK))

    def prepare(src, row, first_block, blocks, put):
        for k in range(blocks):
            columns = pl.ds(k * BLOCK, BLOCK)
            masked = src[:, columns] * mask[row, pl.ds(first_block + k, 1), :]
            put(columns, *split(masked))

    def put_at(place):
        def put(columns, h, l):
            high[place, :, columns] = h
            low[place, :, columns] = l

        return put

    def keep(g, value):
        u[g] = value.reshape(NR, ROWS, BLOCK)

    def send(src, dst, send_sem, recv_sem, device):
        pltpu.make_async_remote_copy(
            src_ref=src, dst_ref=dst, send_sem=send_sem, recv_sem=recv_sem,
            device_id=device, device_id_type=MESH,
        ).start()

    def wait_slots(buffer, count, sem):
        part = buffer.at[pl.ds(0, count)]
        pltpu.make_async_copy(part, part, sem).wait()

    def either(condition, small, large, buffer, sem):
        @pl.when(condition)
        def _():
            wait_slots(buffer, small, sem)

        @pl.when(jnp.logical_not(condition))
        def _():
            wait_slots(buffer, large, sem)

    def forward(g, row):
        for j in range(NR):
            to = scanner(j)

            @pl.when(jnp.logical_or(row != x, to != q))
            def _():
                send(u.at[g, j], f.at[g, q], fwd_send.at[g], fwd_recv.at[g], at(row, y, to))

        @pl.when(jnp.logical_and(scans, row == x))
        def _():
            f[g, q] = u[g, slot]

    def scan(g):
        total = f[g, 0]
        e[g, 0] = total
        for s in range(1, NQ):
            total = total + f[g, s]
            e[g, s] = total
        tot[g] = total
        for k in range(1, NY):
            @pl.when(k > y)
            def _():
                send(tot.at[g], yb.at[g, y], y_send.at[g, k], y_recv.at[g, y], at(x, k, q))

    def total_waits(g, earlier):
        for k in range(NY):
            @pl.when(k < y if earlier else k > y)
            def _():
                sem = y_recv if earlier else y_send
                pltpu.make_async_copy(yb.at[g, k], yb.at[g, k], sem.at[g, k]).wait()

    def add_earlier(g):
        total_waits(g, True)
        before = jnp.zeros((ROWS, BLOCK), jnp.float32)
        for k in range(NY):
            before = before + jnp.where(k < y, yb[g, k], 0.0)
        for s in range(NQ):
            e[g, s] = e[g, s] + before

    loads[0].wait()
    prepare(own, x, 0, 8, put_at(c))
    keep(OWN, product(high[c], low[c], high[c], low[c]))
    forward(OWN, x)

    @pl.when(scans)
    def _():
        wait_slots(f.at[OWN], NQ - 1, fwd_recv.at[OWN])
        scan(OWN)

    first.wait_recv()
    third.wait_recv()
    for k in range(4):
        columns = pl.ds(k * BLOCK, BLOCK)
        block = (x // 2) * 4 + k
        from_near = near[:, pl.ds(pl.multiple_of(block * BLOCK, BLOCK), BLOCK)]
        for place, (value, row) in enumerate(((from_near, behind), (far[:, columns], ahead))):
            h, l = split(value * mask[row, pl.ds(block, 1), :])
            side = c if place == 0 else 1 - c
            fhigh[side, :, columns] = h
            flow[side, :, columns] = l
    keep(FAR, product(fhigh[0], flow[0], fhigh[1], flow[1]))
    forward(FAR, x)

    second.wait_recv()
    prepare(near, behind, 0, 8, put_at(1 - c))
    keep(NEAR, product(high[0], low[0], high[1], low[1]))
    forward(NEAR, lax.rem(x + c, NX))

    @pl.when(scans)
    def _():
        add_earlier(OWN)
        for p in range(NQ):
            @pl.when(p != q)
            def _():
                send(e.at[OWN, p], ret.at[0, slot], ret_send.at[0], ret_recv.at[0], at(x, y, p))

        ret[0, slot] = e[OWN, q]
        wait_slots(f.at[FAR], NQ - 1, fwd_recv.at[FAR])
        scan(FAR)
        either(c == 0, NQ - 1, NQ, f.at[NEAR], fwd_recv.at[NEAR])
        scan(NEAR)
        add_earlier(FAR)
        for p in range(NQ):
            send(e.at[FAR, p], ret.at[2, slot], rt_send.at[1], ret_recv.at[2], at(down, y, p))
            send(e.at[FAR, p], rt.at[1, slot], rt_send.at[2], rt_recv.at[1], at(up, y, p))
        add_earlier(NEAR)
        for p in range(NQ):
            @pl.when(p != q)
            def _():
                send(e.at[NEAR, p], ret.at[1, slot], ret_send.at[1], ret_recv.at[1], at(x, y, p))

            send(e.at[NEAR, p], rt.at[0, slot], rt_send.at[0], rt_recv.at[0], at(down, y, p))
        ret[1, slot] = e[NEAR, q]

    loads[3].wait()
    loads[4].wait()
    either(scans, NR - 1, NR, ret.at[0], ret_recv.at[0])
    wait_slots(ret.at[2], NR, ret_recv.at[2])
    wait_slots(rt.at[1], NR, rt_recv.at[1])
    either(scans, NR - 1, NR, ret.at[1], ret_recv.at[1])
    wait_slots(rt.at[0], NR, rt_recv.at[0])
    square = (BLOCK, BLOCK)
    slots = (NR, ROWS, BLOCK)
    ret[3] = rt[0].reshape(square).T.reshape(slots)
    ret[2] = ret[2] + rt[1].reshape(square).T.reshape(slots)
    for s in range(4):
        away = lax.rem(x - targets_ref[s // 2, s % 2] + NX, NX)
        columns = pl.ds(s * BLOCK, BLOCK)
        out_ref[0, :, columns] = pan[:, columns] - ret[away].reshape(square)

    first.wait_send()
    second.wait_send()
    third.wait_send()
    for g in (OWN, FAR):
        either(scans, NR - 1, NR, u.at[g], fwd_send.at[g])
    either(jnp.logical_and(scans, c == 0), NR - 1, NR, u.at[NEAR], fwd_send.at[NEAR])

    @pl.when(scans)
    def _():
        for g in (OWN, NEAR, FAR):
            total_waits(g, False)
        for g in (OWN, NEAR):
            wait_slots(e.at[g], NQ - 1, ret_send.at[g])
        wait_slots(e.at[NEAR], NQ, rt_send.at[0])
        wait_slots(e.at[FAR], NQ, rt_send.at[1])
        wait_slots(e.at[FAR], NQ, rt_send.at[2])


def body(factor, pattern, order, targets, panels):
    vm, sem = pltpu.VMEM, pltpu.SemaphoreType.DMA
    f32, bf16 = jnp.float32, jnp.bfloat16
    rows, width = factor.shape[1:]
    tile = (ROWS, BLOCK)
    return pl.pallas_call(
        kernel,
        out_shape=jax.ShapeDtypeStruct((1, *panels.shape), f32),
        in_specs=[pl.BlockSpec(memory_space=pl.ANY) for _ in range(5)],
        out_specs=pl.BlockSpec(memory_space=pltpu.VMEM),
        scratch_shapes=[
            pltpu.SMEM((128,), jnp.int32), pltpu.SMEM((2, 2), jnp.int32), vm((NX, 8, BLOCK), jnp.int32),
            vm((rows, width), f32), vm((rows, width), f32), vm((rows, width // 2), f32),
            vm((2, rows, width), bf16), vm((2, rows, width), bf16),
            vm((2, rows, width // 2), bf16), vm((2, rows, width // 2), bf16),
            vm((NX, 8, BLOCK), f32), vm(panels.shape, f32),
            vm((3, NR, *tile), f32), vm((3, NQ, *tile), f32), vm((3, *tile), f32),
            vm((3, NY, *tile), f32), vm((3, NQ, *tile), f32), vm((4, NR, *tile), f32), vm((2, NR, *tile), f32),
            sem((3,)), sem((3,)), sem((5,)),
            sem((3,)), sem((3,)), sem((3, NY)), sem((3, NY)), sem((2,)), sem((3,)), sem((3,)), sem((2,)),
        ],
        compiler_params=pltpu.CompilerParams(
            collective_id=0, has_side_effects=True, vmem_limit_bytes=60 * 2**20
        ),
        name="fan_in",
    )(order, targets, jnp.transpose(pattern, (1, 2, 0)), factor, panels)


def solution(mesh):
    torus = Mesh(mesh.devices.reshape(NY, NZ, NC, NX), (*COL, "x"))
    in_specs = (P(COL, "x", None), P(), P(), P(), P("x", None))
    return jax.shard_map(
        body, mesh=torus, in_specs=in_specs, out_specs=P(COL, "x", None), check_vma=False
    )
```

```python
import jax
import jax.numpy as jnp
from jax import lax
from jax.experimental import pallas as pl
from jax.experimental.pallas import tpu as pltpu
from jax.sharding import Mesh
from jax.sharding import PartitionSpec as P

BLOCK = 128
NX, NY, NZ, NC = 4, 8, 8, 2
NQ = NZ * NC
NR = 16
ROWS = BLOCK // NR
BASE = 0 if NR == NQ else NQ - NR // 2
MESH = pl.DeviceIdType.MESH
COL = ("y", "z", "core")
OWN, NEAR, FAR = 0, 1, 2
FARTHEST_FIRST = (6, 7, 8, 9, 4, 5, 10, 11, 2, 3, 12, 13, 0, 1, 14, 15)


def split(value):
    high = value.astype(jnp.bfloat16)
    return high, (value - high.astype(jnp.float32)).astype(jnp.bfloat16)


def product(ah, al, bh, bl):
    def dot(a, b):
        return lax.dot_general(
            a, b, (((1,), (1,)), ((), ())), preferred_element_type=jnp.float32
        )

    return dot(ah, bh) + (dot(ah, bl) + dot(al, bh))


def kernel(
    order_hbm, pattern_hbm, factor_hbm, ret,
    order_ref, pattern_ref, own, near, far, high, low, fhigh, flow, mask,
    u, f, g, tot, yb, e,
    heavy_send, heavy_recv, local_sem,
    fwd_send, fwd_recv, y_send, y_recv, ret_send, ret_recv, rt_send, rt_recv,
):
    x, y, z, c = (lax.axis_index(a) for a in ("x", "y", "z", "core"))
    q = z * NC + c
    slot = lax.rem(q + NQ - BASE, NQ)
    scans = slot < NR
    joins = lax.rem(z, 2) == x // 2
    position = y * NQ + q
    up, down, across = (lax.rem(x + k, NX) for k in (1, 3, 2))
    ahead = lax.rem(x + 1 + 2 * c, NX)
    behind = lax.rem(x + 3 + 2 * c, NX)

    def at(x_, y_, q_):
        return (y_, q_ // NC, lax.rem(q_, NC), x_)

    def scanner(j):
        return lax.rem(j + BASE, NQ)

    def half(row):
        return pl.ds(pl.multiple_of((row // 2) * 512, 512), 512)

    def other(row):
        return pl.ds(pl.multiple_of((1 - row // 2) * 512, 512), 512)

    loads = [
        pltpu.make_async_copy(a, b, local_sem.at[i])
        for i, (a, b) in enumerate((
            (factor_hbm.at[0], own), (order_hbm, order_ref), (pattern_hbm, pattern_ref),
        ))
    ]
    for load in loads:
        load.start()

    barrier = pltpu.get_barrier_semaphore()

    def greet(device):
        pl.semaphore_signal(barrier, inc=1, device_id=device, device_id_type=MESH)

    for k in range(1, NX):
        greet(at(lax.rem(x + k, NX), y, q))
    for k in range(1, NQ):
        greet(at(x, y, lax.rem(q + k, NQ)))
    for k in range(1, NY):
        greet(at(x, lax.rem(y + k, NY), q))

    @pl.when(scans)
    def _():
        for k in range(NZ):
            greet(at(down, y, k * NC + 1))

    pl.semaphore_wait(barrier, NX + NQ + NY - 3 + c * NR)

    def exchange(src, dst, i, row):
        return pltpu.make_async_remote_copy(
            src_ref=src, dst_ref=dst, send_sem=heavy_send.at[i], recv_sem=heavy_recv.at[i],
            device_id=at(row, y, q), device_id_type=MESH,
        )

    first = exchange(factor_hbm.at[0, :, half(ahead)], near.at[:, half(ahead)], 0, ahead)
    second = exchange(factor_hbm.at[0, :, other(ahead)], near.at[:, other(ahead)], 1, ahead)
    third = exchange(factor_hbm.at[0, :, half(behind)], far, 2, behind)
    first.start()
    third.start()
    second.start()

    loads[1].wait()
    loads[2].wait()
    lanes = lax.broadcasted_iota(jnp.int32, (8, BLOCK), 1)
    picked = lanes == order_ref[position]
    for j in range(NX):
        kept = jnp.where(picked, pattern_ref[j], 0).astype(jnp.float32)
        mask[j] = jnp.broadcast_to(jnp.sum(kept, axis=1, keepdims=True), (8, BLOCK))

    def prepare(src, row, first_block, blocks, put):
        for k in range(blocks):
            columns = pl.ds(pl.multiple_of((first_block + k) * BLOCK, BLOCK), BLOCK)
            masked = src[:, columns] * mask[row, pl.ds(first_block + k, 1), :]
            put(columns, *split(masked))

    def put_at(place):
        def put(columns, h, l):
            high[place, :, columns] = h
            low[place, :, columns] = l

        return put

    def keep(b, value):
        u[b] = value.reshape(NR, ROWS, BLOCK)

    def send(src, dst, send_sem, recv_sem, device):
        pltpu.make_async_remote_copy(
            src_ref=src, dst_ref=dst, send_sem=send_sem, recv_sem=recv_sem,
            device_id=device, device_id_type=MESH,
        ).start()

    def wait_slots(buffer, count, sem):
        part = buffer.at[pl.ds(0, count)]
        pltpu.make_async_copy(part, part, sem).wait()

    def either(condition, small, large, buffer, sem):
        @pl.when(condition)
        def _():
            wait_slots(buffer, small, sem)

        @pl.when(jnp.logical_not(condition))
        def _():
            wait_slots(buffer, large, sem)

    def forward(b, row):
        for j in FARTHEST_FIRST:
            to = scanner(j)

            @pl.when(jnp.logical_or(row != x, to != q))
            def _():
                send(u.at[b, j], f.at[b, q], fwd_send.at[b], fwd_recv.at[b], at(row, y, to))

        @pl.when(jnp.logical_and(scans, row == x))
        def _():
            f[b, q] = u[b, slot]

    def scan(b, part):
        total = part(0)
        e[b, 0] = total
        for s in range(1, NQ):
            total = total + part(s)
            e[b, s] = total
        tot[b] = total
        for k in range(1, NY):
            @pl.when(k > y)
            def _():
                send(tot.at[b], yb.at[b, y], y_send.at[b, k], y_recv.at[b, y], at(x, k, q))

    def total_waits(b, earlier):
        for k in range(NY):
            @pl.when(k < y if earlier else k > y)
            def _():
                sem = y_recv if earlier else y_send
                pltpu.make_async_copy(yb.at[b, k], yb.at[b, k], sem.at[b, k]).wait()

    def add_earlier(b):
        total_waits(b, True)
        before = jnp.zeros((ROWS, BLOCK), jnp.float32)
        for k in range(NY):
            before = before + jnp.where(k < y, yb[b, k], 0.0)
        for s in range(NQ):
            e[b, s] = e[b, s] + before

    loads[0].wait()
    prepare(own, x, 0, 8, put_at(c))
    keep(OWN, product(high[c], low[c], high[c], low[c]))
    forward(OWN, x)

    @pl.when(scans)
    def _():
        wait_slots(f.at[OWN], NQ - 1, fwd_recv.at[OWN])
        scan(OWN, lambda s: f[OWN, s])

    first.wait_recv()
    third.wait_recv()
    for k in range(4):
        columns = pl.ds(k * BLOCK, BLOCK)
        block = (x // 2) * 4 + k
        from_near = near[:, pl.ds(pl.multiple_of(block * BLOCK, BLOCK), BLOCK)]
        for value, row in ((from_near, behind), (far[:, columns], ahead)):
            h, l = split(value * mask[row, pl.ds(block, 1), :])
            fhigh[row // 2, :, columns] = h
            flow[row // 2, :, columns] = l
    keep(FAR, product(fhigh[0], flow[0], fhigh[1], flow[1]))
    for j in FARTHEST_FIRST:
        row = jnp.where(lax.rem(j // NC, 2) == x // 2, x, across)

        @pl.when(jnp.logical_or(row != x, j != q))
        def _():
            send(u.at[FAR, j], g.at[x // 2, q], fwd_send.at[FAR], fwd_recv.at[FAR], at(row, y, j))

    @pl.when(joins)
    def _():
        g[x // 2, q] = u[FAR, slot]

    prepare(near, behind, (x // 2) * 4, 4, put_at(1 - c))
    second.wait_recv()
    prepare(near, behind, (1 - x // 2) * 4, 4, put_at(1 - c))
    keep(NEAR, product(high[0], low[0], high[1], low[1]))
    forward(NEAR, lax.rem(x + c, NX))

    @pl.when(scans)
    def _():
        add_earlier(OWN)
        for p in range(NQ):
            @pl.when(p != q)
            def _():
                send(e.at[OWN, p], ret.at[0, slot], ret_send.at[0], ret_recv.at[0], at(x, y, p))

        keep_own = pltpu.make_async_copy(e.at[OWN, q], ret.at[0, slot], local_sem.at[3])
        keep_own.start()

        @pl.when(joins)
        def _():
            flat = g.reshape(2 * NQ, ROWS, BLOCK)
            wait_slots(flat, 2 * NQ - 1, fwd_recv.at[FAR])
            scan(FAR, lambda s: g[0, s] + g[1, s])

        either(c == 0, NQ - 1, NQ, f.at[NEAR], fwd_recv.at[NEAR])
        scan(NEAR, lambda s: f[NEAR, s])

        def far_back(places):
            for p in places:
                send(e.at[FAR, p], ret.at[2, slot], rt_send.at[1], ret_recv.at[2], at(down, y, p))
                send(e.at[FAR, p], ret.at[2, slot], rt_send.at[2], ret_recv.at[2], at(up, y, p))

        def near_back(places):
            for p in places:
                @pl.when(p != q)
                def _():
                    send(e.at[NEAR, p], ret.at[1, slot], ret_send.at[1], ret_recv.at[1], at(x, y, p))

                send(e.at[NEAR, p], ret.at[3, slot], rt_send.at[0], rt_recv.at[0], at(down, y, p))

        @pl.when(joins)
        def _():
            add_earlier(FAR)
            far_back(range(NQ // 2))

        add_earlier(NEAR)
        near_back(range(NQ // 2))

        @pl.when(joins)
        def _():
            far_back(range(NQ // 2, NQ))

        near_back(range(NQ // 2, NQ))
        keep_near = pltpu.make_async_copy(e.at[NEAR, q], ret.at[1, slot], local_sem.at[4])
        keep_near.start()
        keep_own.wait()
        keep_near.wait()

    either(scans, NR - 1, NR, ret.at[0], ret_recv.at[0])
    wait_slots(ret.at[2], NR, ret_recv.at[2])
    either(scans, NR - 1, NR, ret.at[1], ret_recv.at[1])
    wait_slots(ret.at[3], NR, rt_recv.at[0])

    first.wait_send()
    second.wait_send()
    third.wait_send()
    wait_slots(u.at[OWN], NR - 1, fwd_send.at[OWN])
    either(joins, NR - 1, NR, u.at[FAR], fwd_send.at[FAR])
    either(jnp.logical_and(scans, c == 0), NR - 1, NR, u.at[NEAR], fwd_send.at[NEAR])

    @pl.when(scans)
    def _():
        for b in (OWN, NEAR):
            total_waits(b, False)
        for b in (OWN, NEAR):
            wait_slots(e.at[b], NQ - 1, ret_send.at[b])
        wait_slots(e.at[NEAR], NQ, rt_send.at[0])

        @pl.when(joins)
        def _():
            total_waits(FAR, False)
            wait_slots(e.at[FAR], NQ, rt_send.at[1])
            wait_slots(e.at[FAR], NQ, rt_send.at[2])


def finish(targets_hbm, ret_hbm, panels_hbm, out_hbm, targets_ref, ret, pan, out, sems, out_sems):
    x = lax.axis_index("x")
    square = (BLOCK, BLOCK)
    loads = [pltpu.make_async_copy(ret_hbm.at[k], ret.at[k], sems.at[k]) for k in range(4)]
    loads.append(pltpu.make_async_copy(panels_hbm, pan, sems.at[4]))
    loads.append(pltpu.make_async_copy(targets_hbm, targets_ref, sems.at[5]))
    for load in loads:
        load.start()
    for load in loads:
        load.wait()
    ret[3] = ret[3].reshape(square).T.reshape(ret.shape[1:])
    pair = ret[2].reshape(square)
    ret[2] = jnp.where(x < 2, pair, pair.T).reshape(ret.shape[1:])
    stores = []
    for s in range(4):
        away = lax.rem(x - targets_ref[s // 2, s % 2] + NX, NX)
        columns = pl.ds(s * BLOCK, BLOCK)
        out[:, columns] = pan[:, columns] - ret[away].reshape(square)
        stores.append(pltpu.make_async_copy(out.at[:, columns], out_hbm.at[0, :, columns], out_sems.at[s]))
        stores[-1].start()
    for store in stores:
        store.wait()


def body(factor, pattern, order, targets, panels):
    vm, sem = pltpu.VMEM, pltpu.SemaphoreType.DMA
    f32, bf16 = jnp.float32, jnp.bfloat16
    rows, width = factor.shape[1:]
    tile = (ROWS, BLOCK)
    ret = pl.pallas_call(
        kernel,
        out_shape=jax.ShapeDtypeStruct((4, NR, *tile), f32),
        in_specs=[pl.BlockSpec(memory_space=pl.ANY) for _ in range(3)],
        out_specs=pl.BlockSpec(memory_space=pl.ANY),
        scratch_shapes=[
            pltpu.SMEM((128,), jnp.int32), vm((NX, 8, BLOCK), jnp.int32),
            vm((rows, width), f32), vm((rows, width), f32), vm((rows, width // 2), f32),
            vm((2, rows, width), bf16), vm((2, rows, width), bf16),
            vm((2, rows, width // 2), bf16), vm((2, rows, width // 2), bf16), vm((NX, 8, BLOCK), f32),
            vm((3, NR, *tile), f32), vm((2, NQ, *tile), f32), vm((2, NQ, *tile), f32), vm((3, *tile), f32),
            vm((3, NY, *tile), f32), vm((3, NQ, *tile), f32),
            sem((3,)), sem((3,)), sem((5,)),
            sem((3,)), sem((3,)), sem((3, NY)), sem((3, NY)), sem((2,)), sem((3,)), sem((3,)), sem((2,)),
        ],
        compiler_params=pltpu.CompilerParams(
            collective_id=0, has_side_effects=True, vmem_limit_bytes=60 * 2**20
        ),
        name="fan_in",
    )(order, jnp.transpose(pattern, (1, 2, 0)), factor)
    return pl.pallas_call(
        finish,
        out_shape=jax.ShapeDtypeStruct((1, *panels.shape), f32),
        in_specs=[pl.BlockSpec(memory_space=pl.ANY) for _ in range(3)],
        out_specs=pl.BlockSpec(memory_space=pl.ANY),
        scratch_shapes=[
            pltpu.SMEM((2, 2), jnp.int32),
            vm((4, NR, *tile), f32), vm(panels.shape, f32), vm(panels.shape, f32), sem((6,)), sem((4,)),
        ],
        compiler_params=pltpu.CompilerParams(vmem_limit_bytes=60 * 2**20),
        name="finish",
    )(targets, ret, panels)


def solution(mesh):
    torus = Mesh(mesh.devices.reshape(NY, NZ, NC, NX), (*COL, "x"))
    in_specs = (P(COL, "x", None), P(), P(), P(), P("x", None))
    return jax.shard_map(
        body, mesh=torus, in_specs=in_specs, out_specs=P(COL, "x", None), check_vma=False
    )
```

```python
import jax
import jax.numpy as jnp
from jax import lax
from jax.experimental import pallas as pl
from jax.experimental.pallas import tpu as pltpu
from jax.sharding import Mesh
from jax.sharding import PartitionSpec as P

BLOCK = 128
NX, NY, NZ, NC = 4, 8, 8, 2
NQ = NZ * NC
NR = 16
ROWS = BLOCK // NR
BASE = 0 if NR == NQ else NQ - NR // 2
MESH = pl.DeviceIdType.MESH
COL = ("y", "z", "core")
OWN, NEAR, FAR, REST = 0, 1, 2, 3
QUARTER = 256
FARTHEST_FIRST = (6, 7, 8, 9, 4, 5, 10, 11, 2, 3, 12, 13, 0, 1, 14, 15)


def split(value):
    high = value.astype(jnp.bfloat16)
    return high, (value - high.astype(jnp.float32)).astype(jnp.bfloat16)


def product(ah, al, bh, bl):
    def dot(a, b):
        return lax.dot_general(
            a, b, (((1,), (1,)), ((), ())), preferred_element_type=jnp.float32
        )

    return dot(ah, bh) + (dot(ah, bl) + dot(al, bh))


def kernel(
    order_hbm, pattern_hbm, factor_hbm, ret,
    order_ref, pattern_ref, own, near, far, high, low, fhigh, flow, rhigh, rlow, mask,
    u, f, n, g, tot, yb, e,
    heavy_send, heavy_recv, local_sem,
    fwd_send, fwd_recv, y_send, y_recv, ret_send, ret_recv, rt_send, rt_recv,
):
    x, y, z, c = (lax.axis_index(a) for a in ("x", "y", "z", "core"))
    q = z * NC + c
    slot = lax.rem(q + NQ - BASE, NQ)
    scans = slot < NR
    joins = lax.rem(z, 2) == x // 2
    position = y * NQ + q
    up, down, across = (lax.rem(x + k, NX) for k in (1, 3, 2))
    ahead = lax.rem(x + 1 + 2 * c, NX)
    behind = lax.rem(x + 3 + 2 * c, NX)

    def at(x_, y_, q_):
        return (y_, q_ // NC, lax.rem(q_, NC), x_)

    def scanner(j):
        return lax.rem(j + BASE, NQ)

    def quarter(k):
        return pl.ds(pl.multiple_of(lax.rem(k, NX) * QUARTER, QUARTER), QUARTER)

    loads = [
        pltpu.make_async_copy(a, b, local_sem.at[i])
        for i, (a, b) in enumerate((
            (factor_hbm.at[0], own), (order_hbm, order_ref), (pattern_hbm, pattern_ref),
        ))
    ]
    for load in loads:
        load.start()

    barrier = pltpu.get_barrier_semaphore()

    def greet(device):
        pl.semaphore_signal(barrier, inc=1, device_id=device, device_id_type=MESH)

    for k in range(1, NX):
        greet(at(lax.rem(x + k, NX), y, q))
    for k in range(1, NQ):
        greet(at(x, y, lax.rem(q + k, NQ)))
    for k in range(1, NY):
        greet(at(x, lax.rem(y + k, NY), q))

    loads[0].wait()
    pl.semaphore_wait(barrier, NX + NQ + NY - 3)

    def exchange(src, dst, i, row):
        return pltpu.make_async_remote_copy(
            src_ref=src, dst_ref=dst, send_sem=heavy_send.at[i], recv_sem=heavy_recv.at[i],
            device_id=at(row, y, q), device_id_type=MESH,
        )

    near_parts = [
        exchange(own.at[:, quarter(ahead + k)], near.at[:, quarter(ahead + k)], i, ahead)
        for i, k in enumerate((0, 1, 2 + c))
    ]
    far_parts = [
        exchange(own.at[:, quarter(behind + k)], far.at[:, pl.ds(k * QUARTER, QUARTER)], 3 + k, behind)
        for k in range(2)
    ]
    for part in (near_parts[0], far_parts[0], near_parts[1], far_parts[1], near_parts[2]):
        part.start()

    loads[1].wait()
    loads[2].wait()
    lanes = lax.broadcasted_iota(jnp.int32, (8, BLOCK), 1)
    picked = lanes == order_ref[position]
    for j in range(NX):
        kept = jnp.where(picked, pattern_ref[j], 0).astype(jnp.float32)
        mask[j] = jnp.broadcast_to(jnp.sum(kept, axis=1, keepdims=True), (8, BLOCK))

    def prepare(src, row, first_block, blocks, put):
        for k in range(blocks):
            columns = pl.ds(pl.multiple_of((first_block + k) * BLOCK, BLOCK), BLOCK)
            masked = src[:, columns] * mask[row, pl.ds(first_block + k, 1), :]
            put(columns, *split(masked))

    def put_at(place):
        def put(columns, h, l):
            high[place, :, columns] = h
            low[place, :, columns] = l

        return put

    def keep(b, value):
        u[b] = value.reshape(NR, ROWS, BLOCK)

    def send(src, dst, send_sem, recv_sem, device):
        pltpu.make_async_remote_copy(
            src_ref=src, dst_ref=dst, send_sem=send_sem, recv_sem=recv_sem,
            device_id=device, device_id_type=MESH,
        ).start()

    def wait_slots(buffer, count, sem):
        part = buffer.at[pl.ds(0, count)]
        pltpu.make_async_copy(part, part, sem).wait()

    def either(condition, small, large, buffer, sem):
        @pl.when(condition)
        def _():
            wait_slots(buffer, small, sem)

        @pl.when(jnp.logical_not(condition))
        def _():
            wait_slots(buffer, large, sem)

    def forward(b, to, row):
        for j in FARTHEST_FIRST:
            @pl.when(jnp.logical_or(row != x, j != q))
            def _():
                send(u.at[b, j], to.at[q], fwd_send.at[b], fwd_recv.at[NEAR if b == REST else b], at(row, y, j))

        @pl.when(row == x)
        def _():
            to[q] = u[b, slot]

    def scan(b, part):
        parts = [part(s) for s in range(NQ)]
        level = parts
        while len(level) > 1:
            level = [level[k] + level[k + 1] for k in range(0, len(level), 2)]
        tot[b] = level[0]
        for k in range(1, NY):
            @pl.when(k > y)
            def _():
                send(tot.at[b], yb.at[b, y], y_send.at[b, k], y_recv.at[b, y], at(x, k, q))

        total = parts[0]
        e[b, 0] = total
        for s in range(1, NQ):
            total = total + parts[s]
            e[b, s] = total

    def total_waits(b, earlier):
        for k in range(NY):
            @pl.when(k < y if earlier else k > y)
            def _():
                sem = y_recv if earlier else y_send
                pltpu.make_async_copy(yb.at[b, k], yb.at[b, k], sem.at[b, k]).wait()

    def add_earlier(b):
        total_waits(b, True)
        before = jnp.zeros((ROWS, BLOCK), jnp.float32)
        for k in range(NY):
            before = before + jnp.where(k < y, yb[b, k], 0.0)
        for s in range(NQ):
            e[b, s] = e[b, s] + before

    prepare(own, x, 0, 8, put_at(c))
    keep(OWN, product(high[c], low[c], high[c], low[c]))
    forward(OWN, f, x)

    @pl.when(scans)
    def _():
        wait_slots(f, NQ - 1, fwd_recv.at[OWN])
        scan(OWN, lambda s: f[s])

    def masked(value, row, block):
        return split(value * mask[row, pl.ds(block, 1), :])

    def prepare_near(k):
        blocks = []
        for i in range(2):
            block = lax.rem(k, NX) * 2 + i
            columns = pl.ds(pl.multiple_of(block * BLOCK, BLOCK), BLOCK)
            h, l = masked(near[:, columns], behind, block)
            high[1 - c, :, columns] = h
            low[1 - c, :, columns] = l
            blocks.append((h, l))
        return blocks

    for k in range(2):
        near_parts[k].wait_recv()
        far_parts[k].wait_recv()
        for i, (h, l) in enumerate(prepare_near(x + k)):
            columns = pl.ds((2 * k + i) * BLOCK, BLOCK)
            fhigh[behind // 2, :, columns] = h
            flow[behind // 2, :, columns] = l
            h, l = masked(far[:, columns], ahead, lax.rem(x + k, NX) * 2 + i)
            fhigh[ahead // 2, :, columns] = h
            flow[ahead // 2, :, columns] = l

            @pl.when(c == k)
            def _():
                rhigh[c, :, pl.ds(i * BLOCK, BLOCK)] = h
                rlow[c, :, pl.ds(i * BLOCK, BLOCK)] = l

    keep(FAR, product(fhigh[0], flow[0], fhigh[1], flow[1]))
    for j in FARTHEST_FIRST:
        row = jnp.where(lax.rem(j // NC, 2) == x // 2, x, across)

        @pl.when(jnp.logical_or(row != x, j != q))
        def _():
            send(u.at[FAR, j], g.at[x // 2, q], fwd_send.at[FAR], fwd_recv.at[FAR], at(row, y, j))

    @pl.when(joins)
    def _():
        g[x // 2, q] = u[FAR, slot]

    rhigh[1 - c] = high[c, :, quarter(x + c)]
    rlow[1 - c] = low[c, :, quarter(x + c)]
    keep(REST, product(rhigh[0], rlow[0], rhigh[1], rlow[1]))
    forward(REST, n.at[1], lax.rem(x + 1 - c, NX))

    def near_on(k):
        columns = quarter(k)
        return product(high[0, :, columns], low[0, :, columns], high[1, :, columns], low[1, :, columns])

    early = near_on(x) + near_on(x + 1)
    near_parts[2].wait_recv()
    prepare_near(x + 2 + c)
    keep(NEAR, early + near_on(x + 2 + c))
    forward(NEAR, n.at[0], lax.rem(x + c, NX))

    @pl.when(scans)
    def _():
        add_earlier(OWN)
        for p in range(NQ):
            @pl.when(p != q)
            def _():
                send(e.at[OWN, p], ret.at[0, slot], ret_send.at[0], ret_recv.at[0], at(x, y, p))

        keep_own = pltpu.make_async_copy(e.at[OWN, q], ret.at[0, slot], local_sem.at[3])
        keep_own.start()

        @pl.when(joins)
        def _():
            flat = g.reshape(2 * NQ, ROWS, BLOCK)
            wait_slots(flat, 2 * NQ - 1, fwd_recv.at[FAR])
            scan(FAR, lambda s: g[0, s] + g[1, s])

        wait_slots(n.reshape(2 * NQ, ROWS, BLOCK), 2 * NQ - 1, fwd_recv.at[NEAR])
        scan(NEAR, lambda s: n[0, s] + n[1, s])

        def far_back(places):
            for p in places:
                send(e.at[FAR, p], ret.at[2, slot], rt_send.at[1], ret_recv.at[2], at(down, y, p))
                send(e.at[FAR, p], ret.at[2, slot], rt_send.at[2], ret_recv.at[2], at(up, y, p))

        def near_back(places):
            for p in places:
                @pl.when(p != q)
                def _():
                    send(e.at[NEAR, p], ret.at[1, slot], ret_send.at[1], ret_recv.at[1], at(x, y, p))

                send(e.at[NEAR, p], ret.at[3, slot], rt_send.at[0], rt_recv.at[0], at(down, y, p))

        @pl.when(joins)
        def _():
            add_earlier(FAR)
            far_back(range(NQ // 2))

        add_earlier(NEAR)
        near_back(range(NQ // 2))

        @pl.when(joins)
        def _():
            far_back(range(NQ // 2, NQ))

        near_back(range(NQ // 2, NQ))
        keep_near = pltpu.make_async_copy(e.at[NEAR, q], ret.at[1, slot], local_sem.at[4])
        keep_near.start()
        keep_own.wait()
        keep_near.wait()

    for part in (*near_parts, *far_parts):
        part.wait_send()
    wait_slots(u.at[OWN], NR - 1, fwd_send.at[OWN])
    either(joins, NR - 1, NR, u.at[FAR], fwd_send.at[FAR])
    either(c == 0, NR - 1, NR, u.at[NEAR], fwd_send.at[NEAR])
    either(c == 1, NR - 1, NR, u.at[REST], fwd_send.at[REST])

    @pl.when(scans)
    def _():
        for b in (OWN, NEAR):
            total_waits(b, False)
        for b in (OWN, NEAR):
            wait_slots(e.at[b], NQ - 1, ret_send.at[b])
        wait_slots(e.at[NEAR], NQ, rt_send.at[0])

        @pl.when(joins)
        def _():
            total_waits(FAR, False)
            wait_slots(e.at[FAR], NQ, rt_send.at[1])
            wait_slots(e.at[FAR], NQ, rt_send.at[2])

    either(scans, NR - 1, NR, ret.at[0], ret_recv.at[0])
    wait_slots(ret.at[2], NR, ret_recv.at[2])
    either(scans, NR - 1, NR, ret.at[1], ret_recv.at[1])
    wait_slots(ret.at[3], NR, rt_recv.at[0])


def finish(targets_hbm, ret_hbm, panels_hbm, out_hbm, targets_ref, ret, pan, out, sems, out_sems):
    x = lax.axis_index("x")
    square = (BLOCK, BLOCK)
    loads = [pltpu.make_async_copy(ret_hbm.at[k], ret.at[k], sems.at[k]) for k in range(4)]
    load_pan = pltpu.make_async_copy(panels_hbm, pan, sems.at[4])
    load_targets = pltpu.make_async_copy(targets_hbm, targets_ref, sems.at[5])
    load_targets.start()
    load_pan.start()
    for load in loads:
        load.start()
    load_targets.wait()
    load_pan.wait()
    stores = []
    for k in range(4):
        loads[k].wait()
        block = ret[k].reshape(square)
        if k == 2:
            block = jnp.where(x < 2, block, block.T)
        elif k == 3:
            block = block.T
        row = lax.rem(x - k + NX, NX)
        place = sum(jnp.where(targets_ref[s // 2, s % 2] == row, s, 0) for s in range(4))
        columns = pl.ds(pl.multiple_of(place * BLOCK, BLOCK), BLOCK)
        out[:, columns] = pan[:, columns] - block
        stores.append(pltpu.make_async_copy(out.at[:, columns], out_hbm.at[0, :, columns], out_sems.at[k]))
        stores[-1].start()
    for store in stores:
        store.wait()


def body(factor, pattern, order, targets, panels):
    vm, sem = pltpu.VMEM, pltpu.SemaphoreType.DMA
    f32, bf16 = jnp.float32, jnp.bfloat16
    rows, width = factor.shape[1:]
    tile = (ROWS, BLOCK)
    ret = pl.pallas_call(
        kernel,
        out_shape=jax.ShapeDtypeStruct((4, NR, *tile), f32),
        in_specs=[pl.BlockSpec(memory_space=pl.ANY) for _ in range(3)],
        out_specs=pl.BlockSpec(memory_space=pl.ANY),
        scratch_shapes=[
            pltpu.SMEM((128,), jnp.int32), vm((NX, 8, BLOCK), jnp.int32),
            vm((rows, width), f32), vm((rows, width), f32), vm((rows, width // 2), f32),
            vm((2, rows, width), bf16), vm((2, rows, width), bf16),
            vm((2, rows, width // 2), bf16), vm((2, rows, width // 2), bf16),
            vm((2, rows, QUARTER), bf16), vm((2, rows, QUARTER), bf16), vm((NX, 8, BLOCK), f32),
            vm((4, NR, *tile), f32), vm((NQ, *tile), f32), vm((2, NQ, *tile), f32), vm((2, NQ, *tile), f32), vm((3, *tile), f32),
            vm((3, NY, *tile), f32), vm((3, NQ, *tile), f32),
            sem((5,)), sem((5,)), sem((5,)),
            sem((4,)), sem((3,)), sem((3, NY)), sem((3, NY)), sem((2,)), sem((3,)), sem((3,)), sem((2,)),
        ],
        compiler_params=pltpu.CompilerParams(
            collective_id=0, has_side_effects=True, vmem_limit_bytes=60 * 2**20
        ),
        name="fan_in",
    )(order, jnp.transpose(pattern, (1, 2, 0)), factor)
    return pl.pallas_call(
        finish,
        out_shape=jax.ShapeDtypeStruct((1, *panels.shape), f32),
        in_specs=[pl.BlockSpec(memory_space=pl.ANY) for _ in range(3)],
        out_specs=pl.BlockSpec(memory_space=pl.ANY),
        scratch_shapes=[
            pltpu.SMEM((2, 2), jnp.int32),
            vm((4, NR, *tile), f32), vm(panels.shape, f32), vm(panels.shape, f32), sem((6,)), sem((4,)),
        ],
        compiler_params=pltpu.CompilerParams(vmem_limit_bytes=60 * 2**20),
        name="finish",
    )(targets, ret, panels)


def solution(mesh):
    torus = Mesh(mesh.devices.reshape(NY, NZ, NC, NX), (*COL, "x"))
    in_specs = (P(COL, "x", None), P(), P(), P(), P("x", None))
    return jax.shard_map(
        body, mesh=torus, in_specs=in_specs, out_specs=P(COL, "x", None), check_vma=False
    )
```

```python
import jax
import jax.numpy as jnp
from jax import lax
from jax.experimental import pallas as pl
from jax.experimental.pallas import tpu as pltpu
from jax.sharding import Mesh
from jax.sharding import PartitionSpec as P

BLOCK = 128
NX, NY, NZ, NC = 4, 8, 8, 2
NQ = NZ * NC
NR = 16
ROWS = BLOCK // NR
BASE = 0 if NR == NQ else NQ - NR // 2
MESH = pl.DeviceIdType.MESH
COL = ("y", "z", "core")
OWN, NEAR, FAR = 0, 1, 2
FARTHEST_FIRST = (6, 7, 8, 9, 4, 5, 10, 11, 2, 3, 12, 13, 0, 1, 14, 15)


def split(value):
    high = value.astype(jnp.bfloat16)
    return high, (value - high.astype(jnp.float32)).astype(jnp.bfloat16)


def product(ah, al, bh, bl):
    def dot(a, b):
        return lax.dot_general(
            a, b, (((1,), (1,)), ((), ())), preferred_element_type=jnp.float32
        )

    return dot(ah, bh) + (dot(ah, bl) + dot(al, bh))


def kernel(
    order_hbm, pattern_hbm, factor_hbm, ret,
    order_ref, pattern_ref, own, near, far, high, low, fhigh, flow, mask,
    u, f, g, tot, yb, e,
    heavy_send, heavy_recv, local_sem,
    fwd_send, fwd_recv, y_send, y_recv, ret_send, ret_recv, rt_send, rt_recv,
):
    x, y, z, c = (lax.axis_index(a) for a in ("x", "y", "z", "core"))
    q = z * NC + c
    slot = lax.rem(q + NQ - BASE, NQ)
    scans = slot < NR
    joins = lax.rem(z, 2) == x // 2
    position = y * NQ + q
    up, down, across = (lax.rem(x + k, NX) for k in (1, 3, 2))
    ahead = lax.rem(x + 1 + 2 * c, NX)
    behind = lax.rem(x + 3 + 2 * c, NX)

    def at(x_, y_, q_):
        return (y_, q_ // NC, lax.rem(q_, NC), x_)

    def scanner(j):
        return lax.rem(j + BASE, NQ)

    def half(row):
        return pl.ds(pl.multiple_of((row // 2) * 512, 512), 512)

    def other(row):
        return pl.ds(pl.multiple_of((1 - row // 2) * 512, 512), 512)

    loads = [
        pltpu.make_async_copy(a, b, local_sem.at[i])
        for i, (a, b) in enumerate((
            (factor_hbm.at[0], own), (order_hbm, order_ref), (pattern_hbm, pattern_ref),
        ))
    ]
    for load in loads:
        load.start()

    barrier = pltpu.get_barrier_semaphore()

    def greet(device):
        pl.semaphore_signal(barrier, inc=1, device_id=device, device_id_type=MESH)

    for k in range(1, NX):
        greet(at(lax.rem(x + k, NX), y, q))
    for k in range(1, NQ):
        greet(at(x, y, lax.rem(q + k, NQ)))
    for k in range(NY - 1):
        @pl.when(k < y)
        def _():
            greet(at(x, k, q))


    loads[0].wait()
    pl.semaphore_wait(barrier, NX + NQ + NY - 3 - y)

    def exchange(src, dst, i, row):
        return pltpu.make_async_remote_copy(
            src_ref=src, dst_ref=dst, send_sem=heavy_send.at[i], recv_sem=heavy_recv.at[i],
            device_id=at(row, y, q), device_id_type=MESH,
        )

    near_parts = [
        exchange(own.at[rows, columns(ahead)], near.at[rows, columns(ahead)], i, ahead)
        for i, (rows, columns) in enumerate((r, k) for k in (half, other) for r in (pl.ds(0, 64), pl.ds(64, 64)))
    ]
    third = exchange(own.at[:, half(behind)], far, 4, behind)
    near_parts[0].start()
    near_parts[1].start()
    third.start()
    near_parts[2].start()
    near_parts[3].start()

    loads[1].wait()
    loads[2].wait()
    lanes = lax.broadcasted_iota(jnp.int32, (8, BLOCK), 1)
    picked = lanes == order_ref[position]
    for j in range(NX):
        kept = jnp.where(picked, pattern_ref[j], 0).astype(jnp.float32)
        mask[j] = jnp.broadcast_to(jnp.sum(kept, axis=1, keepdims=True), (8, BLOCK))

    def prepare(src, row, first_block, blocks, put):
        for k in range(blocks):
            columns = pl.ds(pl.multiple_of((first_block + k) * BLOCK, BLOCK), BLOCK)
            masked = src[:, columns] * mask[row, pl.ds(first_block + k, 1), :]
            put(columns, *split(masked))

    def put_at(place):
        def put(columns, h, l):
            high[place, :, columns] = h
            low[place, :, columns] = l

        return put

    def keep(b, value):
        u[b] = value.reshape(NR, ROWS, BLOCK)

    def send(src, dst, send_sem, recv_sem, device):
        pltpu.make_async_remote_copy(
            src_ref=src, dst_ref=dst, send_sem=send_sem, recv_sem=recv_sem,
            device_id=device, device_id_type=MESH,
        ).start()

    def wait_slots(buffer, count, sem):
        part = buffer.at[pl.ds(0, count)]
        pltpu.make_async_copy(part, part, sem).wait()

    def either(condition, small, large, buffer, sem):
        @pl.when(condition)
        def _():
            wait_slots(buffer, small, sem)

        @pl.when(jnp.logical_not(condition))
        def _():
            wait_slots(buffer, large, sem)

    def forward(b, row):
        for j in FARTHEST_FIRST:
            to = scanner(j)

            @pl.when(jnp.logical_or(row != x, to != q))
            def _():
                send(u.at[b, j], f.at[b, q], fwd_send.at[b], fwd_recv.at[b], at(row, y, to))

        @pl.when(jnp.logical_and(scans, row == x))
        def _():
            f[b, q] = u[b, slot]

    def scan(b, part):
        parts = [part(s) for s in range(NQ)]
        level = parts
        while len(level) > 1:
            level = [level[k] + level[k + 1] for k in range(0, len(level), 2)]
        tot[b] = level[0]
        for k in range(1, NY):
            @pl.when(k > y)
            def _():
                send(tot.at[b], yb.at[b, y], y_send.at[b, k], y_recv.at[b, y], at(x, k, q))

        total = parts[0]
        e[b, 0] = total
        for s in range(1, NQ):
            total = total + parts[s]
            e[b, s] = total

    def total_waits(b, earlier):
        for k in range(NY):
            @pl.when(k < y if earlier else k > y)
            def _():
                sem = y_recv if earlier else y_send
                pltpu.make_async_copy(yb.at[b, k], yb.at[b, k], sem.at[b, k]).wait()

    def add_earlier(b):
        total_waits(b, True)
        before = jnp.zeros((ROWS, BLOCK), jnp.float32)
        for k in range(NY):
            before = before + jnp.where(k < y, yb[b, k], 0.0)
        for s in range(NQ):
            e[b, s] = e[b, s] + before

    prepare(own, x, 0, 8, put_at(c))
    keep(OWN, product(high[c], low[c], high[c], low[c]))
    forward(OWN, x)

    @pl.when(scans)
    def _():
        wait_slots(f.at[OWN], NQ - 1, fwd_recv.at[OWN])
        scan(OWN, lambda s: f[OWN, s])

    near_parts[0].wait_recv()
    near_parts[1].wait_recv()
    third.wait_recv()
    for k in range(4):
        columns = pl.ds(k * BLOCK, BLOCK)
        block = (x // 2) * 4 + k
        from_near = near[:, pl.ds(pl.multiple_of(block * BLOCK, BLOCK), BLOCK)]
        for value, row in ((from_near, behind), (far[:, columns], ahead)):
            h, l = split(value * mask[row, pl.ds(block, 1), :])
            fhigh[row // 2, :, columns] = h
            flow[row // 2, :, columns] = l
    keep(FAR, product(fhigh[0], flow[0], fhigh[1], flow[1]))
    for j in FARTHEST_FIRST:
        row = jnp.where(lax.rem(j // NC, 2) == x // 2, x, across)

        @pl.when(jnp.logical_or(row != x, j != q))
        def _():
            send(u.at[FAR, j], g.at[x // 2, q], fwd_send.at[FAR], fwd_recv.at[FAR], at(row, y, j))

    @pl.when(joins)
    def _():
        g[x // 2, q] = u[FAR, slot]

    prepare(near, behind, (x // 2) * 4, 4, put_at(1 - c))
    near_parts[2].wait_recv()
    near_parts[3].wait_recv()
    prepare(near, behind, (1 - x // 2) * 4, 4, put_at(1 - c))
    keep(NEAR, product(high[0], low[0], high[1], low[1]))
    forward(NEAR, lax.rem(x + c, NX))

    @pl.when(scans)
    def _():
        add_earlier(OWN)
        for p in range(NQ):
            @pl.when(p != q)
            def _():
                send(e.at[OWN, p], ret.at[0, slot], ret_send.at[0], ret_recv.at[0], at(x, y, p))

        keep_own = pltpu.make_async_copy(e.at[OWN, q], ret.at[0, slot], local_sem.at[3])
        keep_own.start()

        @pl.when(joins)
        def _():
            flat = g.reshape(2 * NQ, ROWS, BLOCK)
            wait_slots(flat, 2 * NQ - 1, fwd_recv.at[FAR])
            scan(FAR, lambda s: g[0, s] + g[1, s])

        either(c == 0, NQ - 1, NQ, f.at[NEAR], fwd_recv.at[NEAR])
        scan(NEAR, lambda s: f[NEAR, s])

        def far_back(places):
            for p in places:
                send(e.at[FAR, p], ret.at[2, slot], rt_send.at[1], ret_recv.at[2], at(down, y, p))
                send(e.at[FAR, p], ret.at[2, slot], rt_send.at[2], ret_recv.at[2], at(up, y, p))

        def near_back(places):
            for p in places:
                @pl.when(p != q)
                def _():
                    send(e.at[NEAR, p], ret.at[1, slot], ret_send.at[1], ret_recv.at[1], at(x, y, p))

                send(e.at[NEAR, p], ret.at[3, slot], rt_send.at[0], rt_recv.at[0], at(down, y, p))

        @pl.when(joins)
        def _():
            add_earlier(FAR)
            far_back(range(NQ // 2))

        add_earlier(NEAR)
        near_back(range(NQ // 2))

        @pl.when(joins)
        def _():
            far_back(range(NQ // 2, NQ))

        near_back(range(NQ // 2, NQ))
        keep_near = pltpu.make_async_copy(e.at[NEAR, q], ret.at[1, slot], local_sem.at[4])
        keep_near.start()
        keep_own.wait()
        keep_near.wait()

    near_parts[0].wait_send()
    near_parts[1].wait_send()
    near_parts[2].wait_send()
    near_parts[3].wait_send()
    third.wait_send()
    wait_slots(u.at[OWN], NR - 1, fwd_send.at[OWN])
    either(joins, NR - 1, NR, u.at[FAR], fwd_send.at[FAR])
    either(jnp.logical_and(scans, c == 0), NR - 1, NR, u.at[NEAR], fwd_send.at[NEAR])

    @pl.when(scans)
    def _():
        for b in (OWN, NEAR):
            total_waits(b, False)
        for b in (OWN, NEAR):
            wait_slots(e.at[b], NQ - 1, ret_send.at[b])
        wait_slots(e.at[NEAR], NQ, rt_send.at[0])

        @pl.when(joins)
        def _():
            total_waits(FAR, False)
            wait_slots(e.at[FAR], NQ, rt_send.at[1])
            wait_slots(e.at[FAR], NQ, rt_send.at[2])

    either(scans, NR - 1, NR, ret.at[0], ret_recv.at[0])
    wait_slots(ret.at[2], NR, ret_recv.at[2])
    either(scans, NR - 1, NR, ret.at[1], ret_recv.at[1])
    wait_slots(ret.at[3], NR, rt_recv.at[0])


def finish(targets_hbm, ret_hbm, panels_hbm, out_hbm, targets_ref, ret, pan, out, sems, out_sems):
    x = lax.axis_index("x")
    square = (BLOCK, BLOCK)
    loads = [pltpu.make_async_copy(ret_hbm.at[k], ret.at[k], sems.at[k]) for k in range(4)]
    load_pan = pltpu.make_async_copy(panels_hbm, pan, sems.at[4])
    load_targets = pltpu.make_async_copy(targets_hbm, targets_ref, sems.at[5])
    load_targets.start()
    load_pan.start()
    for load in loads:
        load.start()
    load_targets.wait()
    load_pan.wait()
    stores = []
    for k in range(4):
        loads[k].wait()
        block = ret[k].reshape(square)
        if k == 2:
            block = jnp.where(x < 2, block, block.T)
        elif k == 3:
            block = block.T
        row = lax.rem(x - k + NX, NX)
        place = sum(jnp.where(targets_ref[s // 2, s % 2] == row, s, 0) for s in range(4))
        columns = pl.ds(pl.multiple_of(place * BLOCK, BLOCK), BLOCK)
        out[:, columns] = pan[:, columns] - block
        stores.append(pltpu.make_async_copy(out.at[:, columns], out_hbm.at[0, :, columns], out_sems.at[k]))
        stores[-1].start()
    for store in stores:
        store.wait()


def body(factor, pattern, order, targets, panels):
    vm, sem = pltpu.VMEM, pltpu.SemaphoreType.DMA
    f32, bf16 = jnp.float32, jnp.bfloat16
    rows, width = factor.shape[1:]
    tile = (ROWS, BLOCK)
    ret = pl.pallas_call(
        kernel,
        out_shape=jax.ShapeDtypeStruct((4, NR, *tile), f32),
        in_specs=[pl.BlockSpec(memory_space=pl.ANY) for _ in range(3)],
        out_specs=pl.BlockSpec(memory_space=pl.ANY),
        scratch_shapes=[
            pltpu.SMEM((128,), jnp.int32), vm((NX, 8, BLOCK), jnp.int32),
            vm((rows, width), f32), vm((rows, width), f32), vm((rows, width // 2), f32),
            vm((2, rows, width), bf16), vm((2, rows, width), bf16),
            vm((2, rows, width // 2), bf16), vm((2, rows, width // 2), bf16), vm((NX, 8, BLOCK), f32),
            vm((3, NR, *tile), f32), vm((2, NQ, *tile), f32), vm((2, NQ, *tile), f32), vm((3, *tile), f32),
            vm((3, NY, *tile), f32), vm((3, NQ, *tile), f32),
            sem((5,)), sem((5,)), sem((5,)),
            sem((3,)), sem((3,)), sem((3, NY)), sem((3, NY)), sem((2,)), sem((3,)), sem((3,)), sem((2,)),
        ],
        compiler_params=pltpu.CompilerParams(
            collective_id=0, has_side_effects=True, vmem_limit_bytes=60 * 2**20
        ),
        name="fan_in",
    )(order, jnp.transpose(pattern, (1, 2, 0)), factor)
    return pl.pallas_call(
        finish,
        out_shape=jax.ShapeDtypeStruct((1, *panels.shape), f32),
        in_specs=[pl.BlockSpec(memory_space=pl.ANY) for _ in range(3)],
        out_specs=pl.BlockSpec(memory_space=pl.ANY),
        scratch_shapes=[
            pltpu.SMEM((2, 2), jnp.int32),
            vm((4, NR, *tile), f32), vm(panels.shape, f32), vm(panels.shape, f32), sem((6,)), sem((4,)),
        ],
        compiler_params=pltpu.CompilerParams(vmem_limit_bytes=60 * 2**20),
        name="finish",
    )(targets, ret, panels)


def solution(mesh):
    torus = Mesh(mesh.devices.reshape(NY, NZ, NC, NX), (*COL, "x"))
    in_specs = (P(COL, "x", None), P(), P(), P(), P("x", None))
    return jax.shard_map(
        body, mesh=torus, in_specs=in_specs, out_specs=P(COL, "x", None), check_vma=False
    )
```
